32 devices in a mesh: dp: 4 (over y, x), fsdp: 4 (over z), tensor: 2 (over core).
Axes of the slice: x: 2, y: 2, z: 4, core: 2. Of those that a mesh axis runs over, the one named last changes fastest.
Arguments:
- tokens: bfloat16 [1024, 8192], P(('dp', 'tensor'), 'fsdp'), parts along dimension 0, may hold values from -6 to 6
- gate_weight: bfloat16 [8192, 14336], P('fsdp', 'tensor'), may hold values from -0.09375 to 0.09375
- up_weight: bfloat16 [8192, 14336], P('fsdp', 'tensor'), may hold values from -0.09375 to 0.09375
- down_weight: bfloat16 [14336, 8192], P('tensor', 'fsdp'), may hold values from -0.0625 to 0.0625
- gate_mask: int32 [128, 224], P('fsdp', 'tensor'), may hold values from 0 to 1, as said below
- up_mask: int32 [128, 224], P('fsdp', 'tensor'), may hold values from 0 to 1, as said below
- down_mask: int32 [224, 128], P('tensor', 'fsdp'), may hold values from 0 to 1, as said below
Outputs:
- mixed: bfloat16 [1024, 8192], P(('dp', 'tensor'), 'fsdp'), parts along dimension 0
The draws below stay inside these ranges and needn't reach their ends.
There are 4 independent parts, one for each index of `dp`. The reference program is written for one: setup_inputs(seed, part) draws one part's arguments, and reference() takes and returns one part's arrays. A program takes and returns all parts, laid end to end along the dimension named above; an argument that names none is the same for every part. Nothing has to cross between parts.
Inputs may be any that keep to these rules, and one draw needn't show every extreme that they name: `gate_mask`: 1 keeps a tile, 0 prunes it; each tile column of the gate and up masks and each tile row of the down mask has its own share of kept tiles. `up_mask`: as gate_mask. `down_mask`: as gate_mask, by tile rows.
All inputs are finite; a program needn't handle non-finite values.
Results may differ from the reference program's by a relative error of at most 0.0051.
Values may be sent and summed in bfloat16 or wider, within the bound.
A program may use at most 448 MiB of HBM per device.

```python
import jax
import jax.numpy as jnp

D = 8192
FF = 14336
BLOCK = 64
TOKENS = 256


def tile_mask(key, rows, cols, by_columns):
    first, second = jax.random.split(key)
    if by_columns:
        rates = jax.random.randint(first, (1, cols), 30, 81)
    else:
        rates = jax.random.randint(first, (rows, 1), 30, 81)
    rolls = jax.random.randint(second, (rows, cols), 0, 100)
    return (rolls < rates).astype(jnp.int32)


def draw_gate_mask(key, part):
    key = jax.random.fold_in(key, 11)
    return tile_mask(key, D // BLOCK, FF // BLOCK, True)


def draw_up_mask(key, part):
    key = jax.random.fold_in(key, 12)
    return tile_mask(key, D // BLOCK, FF // BLOCK, True)


def draw_down_mask(key, part):
    key = jax.random.fold_in(key, 13)
    return tile_mask(key, FF // BLOCK, D // BLOCK, False)


def block_scale(rng, dims, cuts, low, top_value):
    def one(position, parts):
        draws = jax.random.uniform(jax.random.fold_in(jax.random.fold_in(rng, 6), position), (parts,), jnp.float32, low / len(cuts), top_value / len(cuts))
        return jnp.repeat(jnp.exp(draws), dims[position] // parts).reshape((-1,) + (1,) * (len(dims) - position - 1))

    factor_of = one(*cuts[0])
    for cut in cuts[1:]:
        factor_of = factor_of * one(*cut)
    return factor_of


def scatter_about(stream_key, extent, width, most, pieces=(), kind=jnp.bfloat16):
    entries = width * jax.random.normal(stream_key, extent, jnp.float32)
    if pieces:
        entries = entries * block_scale(stream_key, extent, pieces, -0.22, 0.18)
    return jnp.clip(entries, -most, most).astype(kind)


def setup_inputs(seed: int = 0, part: int = 0) -> dict:
    key_of = jax.random.split(jax.random.key(seed), 8)
    part_splits = jax.random.split(jax.random.fold_in(key_of[7], part), 8)
    tokens = scatter_about(part_splits[0], (TOKENS, D), 1.0, 6.0, ((0, 2), (1, 4)))
    gate_weight = scatter_about(key_of[1], (D, FF), (D // 2) ** -0.5, 0.09375, ((0, 4), (1, 2)))
    up_weight = scatter_about(key_of[2], (D, FF), (D // 2) ** -0.5, 0.09375, ((0, 4), (1, 2)))
    down_weight = scatter_about(key_of[3], (FF, D), (FF // 2) ** -0.5, 0.0625, ((0, 2), (1, 4)))
    gate_mask = draw_gate_mask(jax.random.fold_in(key_of[7], 71), part)
    up_mask = draw_up_mask(jax.random.fold_in(key_of[7], 71), part)
    down_mask = draw_down_mask(jax.random.fold_in(key_of[7], 71), part)
    return dict(tokens=tokens, gate_weight=gate_weight, up_weight=up_weight, down_weight=down_weight, gate_mask=gate_mask, up_mask=up_mask, down_mask=down_mask)


def apply_mask(weight, mask):
    rows, cols = weight.shape
    tiles = weight.reshape(rows // BLOCK, BLOCK, cols // BLOCK, BLOCK)
    kept = tiles * mask[:, None, :, None].astype(weight.dtype)
    return kept.reshape(rows, cols)


def reference(tokens, gate_weight, up_weight, down_weight, gate_mask, up_mask, down_mask):
    gate_pruned = apply_mask(gate_weight, gate_mask)
    up_pruned = apply_mask(up_weight, up_mask)
    down_pruned = apply_mask(down_weight, down_mask)
    gate = jnp.dot(tokens, gate_pruned, preferred_element_type=jnp.float32)
    up = jnp.dot(tokens, up_pruned, preferred_element_type=jnp.float32)
    hidden = (jax.nn.silu(gate) * up).astype(jnp.bfloat16)
    return jnp.dot(hidden, down_pruned, preferred_element_type=jnp.float32).astype(jnp.bfloat16)
```

```python
import functools

import jax
import jax.numpy as jnp
from jax import lax
from jax.experimental import pallas as pl
from jax.experimental.pallas import tpu as pltpu
from jax.sharding import PartitionSpec as P

BLOCK = 64
MESH = pl.DeviceIdType.MESH
DEPTH = 3
LAG_SUM = 2
LAG_HID = 2
F32 = jnp.float32
BF16 = jnp.bfloat16


def both(lo, value, hi):
    return jnp.logical_and(value >= lo, value < hi)


def kernel(F, T, n, NS, tokens, gate, up, down, gmask, umask, dmask, out,
           tok, wbuf, wm, part, slot, hid, dbuf, dm, dexp, acc, xbuf,
           tok_ssem, tok_rsem, wsem, dsem, rs_ssem, rs_rsem, ag_ssem, ag_rsem, x_ssem, x_rsem):
    z = lax.axis_index("fsdp")
    c = lax.axis_index("tensor")
    last = F - 1
    pos = (z, last - z)
    ahead = (z + 1, z - 1)
    back = (z - 1, z + 1)
    rows = tokens.shape[0]
    depth = gate.shape[0]
    width = down.shape[1]
    tiles = n // BLOCK

    def chunk(d, s):
        return d * NS + s

    def w_copies(d, s):
        b = lax.rem(s, DEPTH)
        cols = pl.ds(pl.multiple_of(chunk(d, s) * n, n), n)
        return (
            pltpu.make_async_copy(gate.at[:, cols], wbuf.at[d, b, :, 0:n], wsem.at[d, b, 0]),
            pltpu.make_async_copy(up.at[:, cols], wbuf.at[d, b, :, n:2 * n], wsem.at[d, b, 1]),
        )

    def d_copy(d, s):
        b = lax.rem(s, DEPTH)
        span = pl.ds(pl.multiple_of(chunk(d, s) * n, n), n)
        return pltpu.make_async_copy(down.at[span, :], dbuf.at[d, b], dsem.at[d, b])

    def rs_copy(d, s):
        return pltpu.make_async_remote_copy(
            src_ref=slot.at[d, s], dst_ref=slot.at[d, s],
            send_sem=rs_ssem.at[d, s], recv_sem=rs_rsem.at[d, s],
            device_id={"fsdp": ahead[d]}, device_id_type=MESH)

    def ag_copy(d, s):
        return pltpu.make_async_remote_copy(
            src_ref=hid.at[d, s], dst_ref=hid.at[d, s],
            send_sem=ag_ssem.at[d, s], recv_sem=ag_rsem.at[d, s],
            device_id={"fsdp": back[d]}, device_id_type=MESH)

    def row_block(i):
        return pl.ds(pl.multiple_of(i * rows, rows), rows)

    def tok_copy(j, owner):
        return pltpu.make_async_remote_copy(
            src_ref=tokens, dst_ref=tok.at[row_block(owner), :],
            send_sem=tok_ssem.at[j - 1], recv_sem=tok_rsem.at[j - 1],
            device_id={"tensor": lax.rem(c + j, T)}, device_id_type=MESH)

    def x_copy(j):
        partner = lax.rem(c + j, T)
        return pltpu.make_async_remote_copy(
            src_ref=acc.at[row_block(partner), :], dst_ref=xbuf.at[j - 1],
            send_sem=x_ssem.at[j - 1], recv_sem=x_rsem.at[j - 1],
            device_id={"tensor": partner}, device_id_type=MESH)

    for s in range(min(DEPTH - 1, NS)):
        for d in range(2):
            for copy in w_copies(d, s):
                copy.start()

    barrier = pltpu.get_barrier_semaphore()
    for j in range(1, T):
        pl.semaphore_signal(barrier, inc=1, device_id={"tensor": lax.rem(c + j, T)}, device_id_type=MESH)

    @pl.when(z > 0)
    def _():
        pl.semaphore_signal(barrier, inc=1, device_id={"fsdp": z - 1}, device_id_type=MESH)

    @pl.when(z < last)
    def _():
        pl.semaphore_signal(barrier, inc=1, device_id={"fsdp": z + 1}, device_id_type=MESH)

    inner = jnp.logical_and(z > 0, z < last)
    ends = 1 if F > 1 else 0

    @pl.when(inner)
    def _():
        pl.semaphore_wait(barrier, T - 1 + 2)

    @pl.when(jnp.logical_not(inner))
    def _():
        pl.semaphore_wait(barrier, T - 1 + ends)

    for j in range(1, T):
        tok_copy(j, c).start()
    for s in range(min(DEPTH - 1, NS)):
        for d in range(2):
            d_copy(d, s).start()
    tok[row_block(c), :] = tokens[...]
    acc[...] = jnp.zeros_like(acc)
    spread = (lax.broadcasted_iota(jnp.int32, (dmask.shape[1], width), 1) // BLOCK
              == lax.broadcasted_iota(jnp.int32, (dmask.shape[1], width), 0))
    dexp[...] = jnp.dot(dmask[...].astype(F32).astype(BF16), spread.astype(F32).astype(BF16),
                        preferred_element_type=F32)
    for j in range(1, T):
        tok_copy(j, lax.rem(c + T - j, T)).wait_recv()

    def first_product(d, s):
        b = lax.rem(s, DEPTH)
        for copy in w_copies(d, s):
            copy.wait()

        @pl.when(s + DEPTH - 1 < NS)
        def _():
            for copy in w_copies(d, s + DEPTH - 1):
                copy.start()

        hit = (lax.broadcasted_iota(jnp.int32, (gmask.shape[1], n), 1) // BLOCK + chunk(d, s) * tiles
               == lax.broadcasted_iota(jnp.int32, (gmask.shape[1], n), 0))
        hit = hit.astype(F32).astype(BF16)
        for k, mask in enumerate((gmask, umask)):
            kept = jnp.dot(mask[...].astype(F32).astype(BF16), hit, preferred_element_type=F32).astype(BF16)
            for r in range(depth // BLOCK):
                span = slice(r * BLOCK, (r + 1) * BLOCK)
                wm[span, k * n:(k + 1) * n] = wbuf[d, b, span, k * n:(k + 1) * n] * kept[r:r + 1, :]
        part[d] = jnp.dot(tok[...], wm[...], preferred_element_type=F32)

    def combine(d, s):
        @pl.when(pos[d] > 0)
        def _():
            rs_copy(d, s).wait_recv()

            @pl.when(pos[d] < last)
            def _():
                slot[d, s] = (part[d] + slot[d, s].astype(F32)).astype(BF16)

            @pl.when(pos[d] == last)
            def _():
                g = part[d, :, 0:n] + slot[d, s, :, 0:n].astype(F32)
                u = part[d, :, n:2 * n] + slot[d, s, :, n:2 * n].astype(F32)
                hid[d, s] = (g / (1.0 + jnp.exp(-g)) * u).astype(BF16)

        @pl.when(pos[d] == 0)
        def _():
            slot[d, s] = part[d].astype(BF16)

        @pl.when(pos[d] < last)
        def _():
            rs_copy(d, s).start()

    def pass_hidden(d, s):
        @pl.when(pos[d] < last)
        def _():
            ag_copy(d, s).wait_recv()

        @pl.when(pos[d] > 0)
        def _():
            ag_copy(d, s).start()

    def second_product(d, s):
        b = lax.rem(s, DEPTH)
        d_copy(d, s).wait()

        @pl.when(s + DEPTH - 1 < NS)
        def _():
            d_copy(d, s + DEPTH - 1).start()

        for i in range(tiles):
            span = slice(i * BLOCK, (i + 1) * BLOCK)
            kept = dexp[pl.ds(chunk(d, s) * tiles + i, 1), :].astype(BF16)
            dm[span, :] = dbuf[d, b, span, :] * kept
        step = min(512, width)
        for i in range(width // step):
            span = slice(i * step, (i + 1) * step)
            acc[:, span] += jnp.dot(hid[d, s], dm[:, span], preferred_element_type=F32)

    def body(t, carry):
        s_sum = [t - LAG_SUM * pos[d] for d in range(2)]
        s_hid = [t - LAG_SUM * last - LAG_HID * (last - pos[d]) for d in range(2)]
        for fn, at in ((first_product, s_sum), (combine, s_sum), (pass_hidden, s_hid), (second_product, s_hid)):
            for d in range(2):
                pl.when(both(0, at[d], NS))(functools.partial(fn, d, at[d]))
        return carry

    lax.fori_loop(0, NS + (LAG_SUM + LAG_HID) * last, body, 0)

    for j in range(1, T):
        x_copy(j).start()

    def drain(s, carry):
        for d in range(2):
            @pl.when(pos[d] < last)
            def _():
                rs_copy(d, s).wait_send()

            @pl.when(pos[d] > 0)
            def _():
                ag_copy(d, s).wait_send()
        return carry

    lax.fori_loop(0, NS, drain, 0)
    for j in range(1, T):
        tok_copy(j, c).wait_send()
        x_copy(j).wait_recv()
    total = acc[row_block(c), :]
    for j in range(1, T):
        total = total + xbuf[j - 1]
    out[...] = total.astype(BF16)
    for j in range(1, T):
        x_copy(j).wait_send()


def solution(mesh):
    F, T = mesh.shape["fsdp"], mesh.shape["tensor"]
    placed = (
        P(("dp", "tensor"), "fsdp"),
        P("fsdp", "tensor"),
        P("fsdp", "tensor"),
        P("tensor", "fsdp"),
        P("fsdp", "tensor"),
        P("fsdp", "tensor"),
        P("tensor", "fsdp"),
    )

    def body(tokens, gate, up, down, gmask, umask, dmask):
        rows, depth = tokens.shape
        units, width = down.shape
        n = 128
        NS = units // (2 * n)
        TT = rows * T
        vm = pltpu.VMEM
        dma = pltpu.SemaphoreType.DMA
        in_vmem = pl.BlockSpec(memory_space=pltpu.VMEM)
        in_hbm = pl.BlockSpec(memory_space=pl.ANY)
        return pl.pallas_call(
            functools.partial(kernel, F, T, n, NS),
            out_shape=jax.ShapeDtypeStruct((rows, width), BF16),
            in_specs=[in_vmem, in_hbm, in_hbm, in_hbm, in_vmem, in_vmem, in_vmem],
            out_specs=in_vmem,
            scratch_shapes=[
                vm((TT, depth), BF16),
                vm((2, DEPTH, depth, 2 * n), BF16),
                vm((depth, 2 * n), BF16),
                vm((2, TT, 2 * n), F32),
                vm((2, NS, TT, 2 * n), BF16),
                vm((2, NS, TT, n), BF16),
                vm((2, DEPTH, n, width), BF16),
                vm((n, width), BF16),
                vm((dmask.shape[0], width), F32),
                vm((TT, width), F32),
                vm((T - 1, rows, width), F32),
                dma((T - 1,)),
                dma((T - 1,)),
                dma((2, DEPTH, 2)),
                dma((2, DEPTH)),
                dma((2, NS)),
                dma((2, NS)),
                dma((2, NS)),
                dma((2, NS)),
                dma((T - 1,)),
                dma((T - 1,)),
            ],
            compiler_params=pltpu.CompilerParams(
                collective_id=0, has_side_effects=True, vmem_limit_bytes=56 * 1024 * 1024),
            cost_estimate=pl.CostEstimate(
                flops=6 * TT * depth * units, bytes_accessed=6 * depth * units, transcendentals=TT * units),
        )(tokens, gate, up, down, gmask, umask, dmask)

    return jax.shard_map(
        body, mesh=mesh, in_specs=placed, out_specs=P(("dp", "tensor"), "fsdp"), check_vma=False
    )
```
